32 devices in a mesh: groups: 2 (over x), col: 16 (over z, y, core).
Axes of the slice: x: 2, y: 2, z: 4, core: 2. Of those that a mesh axis runs over, the one named last changes fastest.
Arguments:
- slab: float32 [2, 2048, 4096], P(None, 'groups', 'col'), parts along dimension 1, may hold values from -6 to 6
- block_on: int32 [16, 32], P('groups', 'col'), parts along dimension 0, may hold values 0 or 1
- block_band: int32 [16, 32], P('groups', 'col'), parts along dimension 0, may hold values from 0 to 3
- band_gain: float32 [4], replicated, may hold values from 0.25 to 2
Outputs:
- spectra: float32 [2, 2048, 4096], P(None, 'groups', 'col'), parts along dimension 1
The draws below stay inside these ranges and needn't reach their ends.
There are 2 independent parts, one for each index of `groups`. The reference program is written for one: setup_inputs(seed, part) draws one part's arguments, and reference() takes and returns one part's arrays. A program takes and returns all parts, laid end to end along the dimension named above; an argument that names none is the same for every part. Nothing has to cross between parts.
All inputs are finite; a program needn't handle non-finite values. No bound on the sum of `block_on` on one device may be relied on, other than what follows from the above.
Results may differ from the reference program's by a relative error of at most 0.00007.
Values sent between devices are 32-bit elements; how exact they have to be, the bound alone decides.
A program may use at most 64 MiB of HBM per device.

```python
import math
import jax
import jax.numpy as jnp
from jax import lax

ROWS = 1024
BLOCK = 128
BANDS = 4
N = 4096
RB = 8
NKB = 32


def touch_ends(entries, stream_key, low, high):
    index_at = [jax.random.randint(jax.random.fold_in(stream_key, axis), (), 0, length) for axis, length in enumerate(entries.shape)]
    main_axis = entries.shape.index(max(entries.shape))
    beside = index_at[:main_axis] + [(index_at[main_axis] + 1) % entries.shape[main_axis]] + index_at[main_axis + 1:]
    return entries.at[tuple(index_at)].set(low).at[tuple(beside)].set(high)


def block_levels(stream_key, shape, cuts, low, high):
    gain, own = 1.0, jax.random.fold_in(stream_key, 6)
    for dim, blocks in cuts:
        steps = jnp.exp(jax.random.uniform(jax.random.fold_in(own, dim), (blocks,), jnp.float32, low / len(cuts), high / len(cuts)))
        gain = gain * jnp.repeat(steps, shape[dim] // blocks).reshape([-1 if axis == dim else 1 for axis in range(len(shape))])
    return gain


def normal_values(stream_key, dims, spread, limit, split=(), held_as=jnp.bfloat16):
    values = jax.random.normal(stream_key, dims, jnp.float32) * spread
    if len(split) > 0:
        values = block_levels(stream_key, dims, split, -0.22, 0.18) * values
    return jnp.clip(values, min=-limit, max=limit).astype(held_as)


def setup_inputs(seed: int = 0, part: int = 0) -> dict:
    splits = jax.random.split(jax.random.key(seed), 5)
    part_splits = jax.random.split(jax.random.fold_in(splits[4], part), 5)
    return {
        "slab": normal_values(part_splits[0], (2, ROWS, N), 1.0, 6.0, ((2, 16),), jnp.float32),
        "block_on": touch_ends((jax.random.randint(part_splits[1], (RB, NKB), 0, 2) < 1).astype(jnp.int32), jax.random.fold_in(part_splits[1], 1), 0, 1),
        "block_band": touch_ends(jax.random.randint(part_splits[2], (RB, NKB), 0, BANDS), jax.random.fold_in(part_splits[2], 1), 0, BANDS - 1).astype(jnp.int32),
        "band_gain": jnp.clip(jnp.exp(jax.random.uniform(splits[3], (BANDS,), jnp.float32, math.log(0.25), math.log(2.0))), 0.25, 2.0),
    }


def reference(slab, block_on, block_band, band_gain):
    signal = lax.complex(slab[0], slab[1])
    spectrum = jnp.fft.fft(signal, axis=-1, norm="ortho")
    stacked_parts = jnp.stack([jnp.real(spectrum), jnp.imag(spectrum)])
    selector = (block_band[..., None] == jnp.arange(BANDS, dtype=jnp.int32)).astype(band_gain.dtype)
    weights = block_on.astype(band_gain.dtype) * jnp.sum(selector * band_gain, axis=-1)
    shaped = stacked_parts.reshape(2, RB, BLOCK, NKB, BLOCK) * weights[None, :, None, :, None]
    return shaped.reshape(2, ROWS, N)
```

```python
import functools
import math

import jax
import jax.numpy as jnp
import ml_dtypes
import numpy as np
from jax import lax
from jax.experimental import pallas as pl
from jax.experimental.pallas import tpu as pltpu
from jax.sharding import PartitionSpec as P

BLOCK = 128
LANES = 128
MESH = pl.DeviceIdType.MESH


def butterflies(planes):
    count = len(planes)
    if count == 1:
        return planes
    even = butterflies(planes[0::2])
    odd = butterflies(planes[1::2])
    low, high = [], []
    for k in range(count // 2):
        er, ei = even[k]
        xr, xi = odd[k]
        if k == 0:
            tr, ti = xr, xi
        elif 4 * k == count:
            tr, ti = xi, -xr
        else:
            c = math.cos(2.0 * math.pi * k / count)
            s = -math.sin(2.0 * math.pi * k / count)
            if 8 * k == count:
                tr, ti = c * (xr + xi), c * (xi - xr)
            elif 8 * k == 3 * count:
                tr, ti = s * (xr - xi), s * (xr + xi)
            else:
                tr, ti = c * xr - s * xi, c * xi + s * xr
        low.append((er + tr, ei + ti))
        high.append((er - tr, ei - ti))
    return low + high


def kernel(
    n, chunks, rows, x_ref, tw_ref, whi_ref, wlo_ref, out_ref,
    recv, mid, spread, done, s1, r1, s2, r2, own1, own2,
):
    me = lax.axis_index("col")
    rows_here = chunks * rows
    width = x_ref.shape[2]

    barrier = pltpu.get_barrier_semaphore()

    def greet(t, carry):
        pl.semaphore_signal(
            barrier, inc=1, device_id={"col": lax.rem(me + t, n)}, device_id_type=MESH
        )
        return carry

    lax.fori_loop(1, n, greet, 0)

    def part_of(ref, owner, c):
        start = pl.multiple_of(owner * rows_here + c * rows, rows)
        return ref.at[:, pl.ds(start, rows), :]

    def first(c, t):
        peer = lax.rem(me + t, n)
        return pltpu.make_async_remote_copy(
            src_ref=part_of(x_ref, peer, c),
            dst_ref=recv.at[c, me],
            send_sem=s1.at[c, t],
            recv_sem=r1.at[c, t],
            device_id={"col": peer},
            device_id_type=MESH,
        )

    def second(c, t):
        peer = lax.rem(me + t, n)
        return pltpu.make_async_remote_copy(
            src_ref=done.at[c, peer],
            dst_ref=part_of(out_ref, me, c),
            send_sem=s2.at[c, t],
            recv_sem=r2.at[c, t],
            device_id={"col": peer},
            device_id_type=MESH,
        )

    def own_in(c):
        return pltpu.make_async_copy(part_of(x_ref, me, c), recv.at[c, me], own1.at[c])

    def own_out(c):
        return pltpu.make_async_copy(done.at[c, me], part_of(out_ref, me, c), own2.at[c])

    for c in range(chunks):
        own_in(c).start()
    pl.semaphore_wait(barrier, n - 1)
    for c in range(chunks):

        def send_first(t, carry, c=c):
            first(c, t).start()
            return carry

        lax.fori_loop(1, n, send_first, 0)

    for c in range(chunks):
        own_in(c).wait()

        def take_first(t, carry, c=c):
            first(c, t).wait_recv()
            return carry

        lax.fori_loop(1, n, take_first, 0)

        def stage_one(g, carry, c=c):
            r0 = pl.multiple_of(g * 8, 8)
            for h in range(width // LANES):
                cols = pl.ds(h * LANES, LANES)
                planes = [
                    (recv[c, d, 0, pl.ds(r0, 8), cols], recv[c, d, 1, pl.ds(r0, 8), cols])
                    for d in range(n)
                ]
                for q, (ar, ai) in enumerate(butterflies(planes)):
                    if q == 0:
                        br, bi = ar, ai
                    else:
                        tr = tw_ref[0, pl.ds(q, 1), cols]
                        ti = tw_ref[1, pl.ds(q, 1), cols]
                        br = ar * tr - ai * ti
                        bi = ar * ti + ai * tr
                    right = pl.ds(width + h * LANES, LANES)
                    mid[q, pl.ds(r0, 8), cols] = br
                    mid[q, pl.ds(r0, 8), right] = -bi
                    mid[q, pl.ds(rows + r0, 8), cols] = bi
                    mid[q, pl.ds(rows + r0, 8), right] = br
            return carry

        lax.fori_loop(0, rows // 8, stage_one, 0)

        def stage_two(q, carry):
            value = mid[q]
            high = value.astype(jnp.bfloat16)
            low = (value - high.astype(jnp.float32)).astype(jnp.bfloat16)
            nt = (((1,), (1,)), ((), ()))
            dot = functools.partial(
                lax.dot_general, dimension_numbers=nt, preferred_element_type=jnp.float32
            )
            total = dot(whi_ref[...], high) + (dot(whi_ref[...], low) + dot(wlo_ref[...], high))
            spread[pl.ds(q, width, stride=n), pl.ds(0, 2 * rows)] = total
            return carry

        if n <= 16:
            for q in range(n):
                stage_two(q, 0)
        else:
            lax.fori_loop(0, n, stage_two, 0)

        def turn(owner):
            start = pl.multiple_of(owner * width, width)
            block = spread[pl.ds(start, width), :].T
            done[c, owner, 0] = block[:rows]
            done[c, owner, 1] = block[rows : 2 * rows]

        def send_second(t, carry, c=c):
            turn(lax.rem(me + t, n))
            second(c, t).start()
            return carry

        lax.fori_loop(1, n, send_second, 0)
        turn(me)
        own_out(c).start()

    for c in range(chunks):
        own_out(c).wait()

        def finish(t, carry, c=c):
            first(c, t).wait_send()
            second(c, t).wait_send()
            second(c, t).wait_recv()
            return carry

        lax.fori_loop(1, n, finish, 0)


def transform(slab, n):
    _, rows_total, width = slab.shape
    length = width * n
    rows_here = rows_total // n
    chunks = 2 if rows_here % 16 == 0 else 1
    rows = rows_here // chunks
    lanes = max(LANES, 2 * rows)
    k0 = np.arange(n)[:, None] * np.arange(width)[None, :]
    angle = 2.0 * np.pi * (k0 % length) / length
    twiddle = np.stack([np.cos(angle), -np.sin(angle)]).astype(np.float32)
    k1 = np.arange(width)[:, None] * np.arange(width)[None, :]
    angle = 2.0 * np.pi * (k1 % width) / width
    table = np.concatenate([np.cos(angle), -np.sin(angle)], axis=1) / math.sqrt(length)
    table_high = table.astype(np.float32).astype(ml_dtypes.bfloat16)
    table_low = (table - table_high.astype(np.float64)).astype(np.float32)
    table_low = table_low.astype(ml_dtypes.bfloat16)
    sem = pltpu.SemaphoreType.DMA
    return pl.pallas_call(
        functools.partial(kernel, n, chunks, rows),
        out_shape=jax.ShapeDtypeStruct(slab.shape, jnp.float32),
        in_specs=[pl.BlockSpec(memory_space=pl.ANY)]
        + [pl.BlockSpec(memory_space=pltpu.VMEM)] * 3,
        out_specs=pl.BlockSpec(memory_space=pl.ANY),
        scratch_shapes=[
            pltpu.VMEM((chunks, n, 2, rows, width), jnp.float32),
            pltpu.VMEM((n, 2 * rows, 2 * width), jnp.float32),
            pltpu.VMEM((length, lanes), jnp.float32),
            pltpu.VMEM((chunks, n, 2, rows, width), jnp.float32),
            sem((chunks, n)),
            sem((chunks, n)),
            sem((chunks, n)),
            sem((chunks, n)),
            sem((chunks,)),
            sem((chunks,)),
        ],
        compiler_params=pltpu.CompilerParams(
            collective_id=0, has_side_effects=True, vmem_limit_bytes=48 * 1024 * 1024
        ),
    )(slab, jnp.asarray(twiddle), jnp.asarray(table_high), jnp.asarray(table_low))


def shards(slab, block_on, block_band, band_gain):
    n = lax.axis_size("col")
    _, rows_total, width = slab.shape
    spectrum = transform(slab, n)
    choose = (block_band[..., None] == jnp.arange(band_gain.shape[0], dtype=jnp.int32)).astype(
        jnp.float32
    )
    weight = block_on.astype(jnp.float32) * jnp.sum(choose * band_gain, axis=-1)
    row_blocks = rows_total // BLOCK
    col_blocks = width // BLOCK
    masked = (
        spectrum.reshape(2, row_blocks, BLOCK, col_blocks, BLOCK) * weight[None, :, None, :, None]
    )
    return masked.reshape(2, rows_total, width)


def solution(mesh):
    placed = (P(None, "groups", "col"), P("groups", "col"), P("groups", "col"), P())
    return jax.shard_map(
        shards, mesh=mesh, in_specs=placed, out_specs=P(None, "groups", "col"), check_vma=False
    )
```

```python
import functools
import math

import jax
import jax.numpy as jnp
import ml_dtypes
import numpy as np
from jax import lax
from jax.experimental import pallas as pl
from jax.experimental.pallas import tpu as pltpu
from jax.sharding import PartitionSpec as P

BLOCK = 128
LANES = 128
MESH = pl.DeviceIdType.MESH


def butterflies(planes):
    count = len(planes)
    if count == 1:
        return planes
    even = butterflies(planes[0::2])
    odd = butterflies(planes[1::2])
    low, high = [], []
    for k in range(count // 2):
        er, ei = even[k]
        xr, xi = odd[k]
        if k == 0:
            tr, ti = xr, xi
        elif 4 * k == count:
            tr, ti = xi, -xr
        else:
            c = math.cos(2.0 * math.pi * k / count)
            s = -math.sin(2.0 * math.pi * k / count)
            if 8 * k == count:
                tr, ti = c * (xr + xi), c * (xi - xr)
            elif 8 * k == 3 * count:
                tr, ti = s * (xr - xi), s * (xr + xi)
            else:
                tr, ti = c * xr - s * xi, c * xi + s * xr
        low.append((er + tr, ei + ti))
        high.append((er - tr, ei - ti))
    return low + high


def kernel(
    n, chunks, rows, x_ref, tw_ref, whi_ref, wlo_ref, out_ref,
    recv, mid, spread, done, s1, r1, s2, r2, own1, own2,
):
    me = lax.axis_index("col")
    rows_here = chunks * rows
    width = x_ref.shape[2]

    barrier = pltpu.get_barrier_semaphore()

    def greet(t, carry):
        pl.semaphore_signal(
            barrier, inc=1, device_id={"col": lax.rem(me + t, n)}, device_id_type=MESH
        )
        return carry

    lax.fori_loop(1, n, greet, 0)

    def part_of(ref, owner, c):
        start = pl.multiple_of(owner * rows_here + c * rows, rows)
        return ref.at[:, pl.ds(start, rows), :]

    def first(c, t):
        peer = lax.rem(me + t, n)
        return pltpu.make_async_remote_copy(
            src_ref=part_of(x_ref, peer, c),
            dst_ref=recv.at[c, me],
            send_sem=s1.at[c, t],
            recv_sem=r1.at[c, t],
            device_id={"col": peer},
            device_id_type=MESH,
        )

    def second(c, t):
        peer = lax.rem(me + t, n)
        return pltpu.make_async_remote_copy(
            src_ref=done.at[c, peer],
            dst_ref=part_of(out_ref, me, c),
            send_sem=s2.at[c, t],
            recv_sem=r2.at[c, t],
            device_id={"col": peer},
            device_id_type=MESH,
        )

    def own_in(c):
        return pltpu.make_async_copy(part_of(x_ref, me, c), recv.at[c, me], own1.at[c])

    def own_out(c):
        return pltpu.make_async_copy(done.at[c, me], part_of(out_ref, me, c), own2.at[c])

    for c in range(chunks):
        own_in(c).start()
    pl.semaphore_wait(barrier, n - 1)
    for c in range(chunks):

        def send_first(t, carry, c=c):
            first(c, t).start()
            return carry

        lax.fori_loop(1, n, send_first, 0)

    for c in range(chunks):
        own_in(c).wait()

        def take_first(t, carry, c=c):
            first(c, t).wait_recv()
            return carry

        lax.fori_loop(1, n, take_first, 0)

        def stage_one(g, carry, c=c):
            r0 = pl.multiple_of(g * 8, 8)
            for h in range(width // LANES):
                cols = pl.ds(h * LANES, LANES)
                planes = [
                    (recv[c, d, 0, pl.ds(r0, 8), cols], recv[c, d, 1, pl.ds(r0, 8), cols])
                    for d in range(n)
                ]
                for q, (ar, ai) in enumerate(butterflies(planes)):
                    if q == 0:
                        br, bi = ar, ai
                    else:
                        tr = tw_ref[0, pl.ds(q, 1), cols]
                        ti = tw_ref[1, pl.ds(q, 1), cols]
                        br = ar * tr - ai * ti
                        bi = ar * ti + ai * tr
                    right = pl.ds(width + h * LANES, LANES)
                    mid[q, pl.ds(r0, 8), cols] = br
                    mid[q, pl.ds(r0, 8), right] = -bi
                    mid[q, pl.ds(rows + r0, 8), cols] = bi
                    mid[q, pl.ds(rows + r0, 8), right] = br
            return carry

        lax.fori_loop(0, rows // 8, stage_one, 0)

        def stage_two(q, carry):
            value = mid[q]
            high = value.astype(jnp.bfloat16)
            low = (value - high.astype(jnp.float32)).astype(jnp.bfloat16)
            nt = (((1,), (1,)), ((), ()))
            dot = functools.partial(
                lax.dot_general, dimension_numbers=nt, preferred_element_type=jnp.float32
            )
            total = dot(whi_ref[...], high) + (dot(whi_ref[...], low) + dot(wlo_ref[...], high))
            spread[pl.ds(q, width, stride=n), pl.ds(0, 2 * rows)] = total
            return carry

        if n <= 16:
            for q in range(n):
                stage_two(q, 0)
        else:
            lax.fori_loop(0, n, stage_two, 0)

        def turn(owner):
            start = pl.multiple_of(owner * width, width)
            block = spread[pl.ds(start, width), :].T
            done[c, owner, 0] = block[:rows]
            done[c, owner, 1] = block[rows : 2 * rows]

        def send_second(t, carry, c=c):
            turn(lax.rem(me + t, n))
            second(c, t).start()
            return carry

        lax.fori_loop(1, n, send_second, 0)
        turn(me)
        own_out(c).start()

    for c in range(chunks):
        own_out(c).wait()

        def finish(t, carry, c=c):
            first(c, t).wait_send()
            second(c, t).wait_send()
            second(c, t).wait_recv()
            return carry

        lax.fori_loop(1, n, finish, 0)


def transform(slab, n):
    _, rows_total, width = slab.shape
    length = width * n
    rows_here = rows_total // n
    chunks = 2 if rows_here % 16 == 0 else 1
    rows = rows_here // chunks
    lanes = max(LANES, 2 * rows)
    sem = pltpu.SemaphoreType.DMA
    return pl.pallas_call(
        functools.partial(kernel, n, chunks, rows),
        out_shape=jax.ShapeDtypeStruct(slab.shape, jnp.float32),
        in_specs=[pl.BlockSpec(memory_space=pl.ANY)]
        + [pl.BlockSpec(memory_space=pltpu.VMEM)] * 3,
        out_specs=pl.BlockSpec(memory_space=pl.ANY),
        scratch_shapes=[
            pltpu.VMEM((chunks, n, 2, rows, width), jnp.float32),
            pltpu.VMEM((n, 2 * rows, 2 * width), jnp.float32),
            pltpu.VMEM((length, lanes), jnp.float32),
            pltpu.VMEM((chunks, n, 2, rows, width), jnp.float32),
            sem((chunks, n)),
            sem((chunks, n)),
            sem((chunks, n)),
            sem((chunks, n)),
            sem((chunks,)),
            sem((chunks,)),
        ],
        compiler_params=pltpu.CompilerParams(
            collective_id=0, has_side_effects=True, vmem_limit_bytes=48 * 1024 * 1024
        ),
    )(slab, *tables(n, width))


def packed_kernel(
    n, groups, chunks, blocks, sub, halves, keep,
    x_ref, on_ref, tw_ref, whi_ref, wlo_ref, out_ref, rest_ref, flag_ref,
    recv, mid, spread, units, send, infos, table,
    s1, r1, s2, r2, si, ri, own1, own2, own3, own4,
):
    me = lax.axis_index("col")
    flat = lax.axis_index("groups") * n + me
    everyone = groups * n
    width = halves * LANES
    per = blocks // chunks
    rows = per * sub
    slots = blocks * halves

    def place(i):
        dev = lax.rem(flat + i, everyone)
        return {"groups": dev // n, "col": lax.rem(dev, n)}

    barrier = pltpu.get_barrier_semaphore()

    def greet(i, carry):
        pl.semaphore_signal(barrier, inc=1, device_id=place(i), device_id_type=MESH)
        return carry

    lax.fori_loop(1, everyone, greet, 0)

    def part(owner, c):
        return x_ref.at[:, pl.ds(c * per, per), owner]

    def first(c, t):
        peer = lax.rem(me + t, n)
        return pltpu.make_async_remote_copy(
            src_ref=part(peer, c),
            dst_ref=recv.at[c, me],
            send_sem=s1.at[c, t],
            recv_sem=r1.at[c, t],
            device_id={"col": peer},
            device_id_type=MESH,
        )

    def second(t):
        peer = lax.rem(me + t, n)
        return pltpu.make_async_remote_copy(
            src_ref=send.at[peer, pl.ds(0, keep)],
            dst_ref=out_ref.at[me],
            send_sem=s2.at[t],
            recv_sem=r2.at[t],
            device_id={"col": peer},
            device_id_type=MESH,
        )

    def tell(i):
        return pltpu.make_async_remote_copy(
            src_ref=infos.at[flat],
            dst_ref=infos.at[flat],
            send_sem=si.at[i],
            recv_sem=ri.at[i],
            device_id=place(i),
            device_id_type=MESH,
        )

    def own_in(c):
        return pltpu.make_async_copy(part(me, c), recv.at[c, me], own1.at[c])

    def own_out():
        return pltpu.make_async_copy(send.at[me, pl.ds(0, keep)], out_ref.at[me], own2)

    def own_rest(owner):
        return pltpu.make_async_copy(
            send.at[owner, pl.ds(keep, slots - keep)], rest_ref.at[owner], own3.at[owner]
        )

    for c in range(chunks):
        own_in(c).start()
    pl.semaphore_wait(barrier, everyone - 1)

    def turned(i):
        return 1 + lax.rem(i + n // 2, n - 1)

    for c in range(chunks):

        def send_first(i, carry, c=c):
            first(c, turned(i)).start()
            return carry

        lax.fori_loop(0, n - 1, send_first, 0)

    ons = [on_ref[u // halves, u % halves] for u in range(slots)]
    ranks, count = [], jnp.int32(0)
    for u in range(slots):
        ranks.append(count)
        count = count + ons[u]
    lane = lax.broadcasted_iota(jnp.int32, (1, LANES), 1)
    row = jnp.where(lane == slots, count, 0)
    for u in range(slots):
        hit = (lane == ranks[u]) & (lane < slots)
        row = row + jnp.where(hit, u * ons[u], 0)
    infos[flat] = row

    def tell_all(i, carry):
        tell(i).start()
        return carry

    lax.fori_loop(1, everyone, tell_all, 0)

    def hear_all(i, carry):
        tell(i).wait_recv()
        return carry

    lax.fori_loop(1, everyone, hear_all, 0)
    fetch = pltpu.make_async_copy(infos, table, own4)
    fetch.start()
    fetch.wait()
    most = jnp.int32(0)
    for i in range(everyone):
        most = jnp.maximum(most, table[i, 0, slots])
    flag_ref[0, 0] = most

    for c in range(chunks):
        own_in(c).wait()

        def take_first(t, carry, c=c):
            first(c, t).wait_recv()
            return carry

        lax.fori_loop(1, n, take_first, 0)

        def stage_one(a, carry, c=c):
            r0 = pl.multiple_of(c * 2 * rows + a * sub, sub)
            for h in range(halves):
                cols = pl.ds(h * LANES, LANES)
                planes = [(recv[c, d, 0, a, :, cols], recv[c, d, 1, a, :, cols]) for d in range(n)]
                for q, (ar, ai) in enumerate(butterflies(planes)):
                    if q == 0:
                        br, bi = ar, ai
                    else:
                        tr = tw_ref[0, pl.ds(q, 1), cols]
                        ti = tw_ref[1, pl.ds(q, 1), cols]
                        br = ar * tr - ai * ti
                        bi = ar * ti + ai * tr
                    right = pl.ds(width + h * LANES, LANES)
                    mid[q, pl.ds(r0, sub), cols] = br
                    mid[q, pl.ds(r0, sub), right] = -bi
                    mid[q, pl.ds(rows + r0, sub), cols] = bi
                    mid[q, pl.ds(rows + r0, sub), right] = br
            return carry

        lax.fori_loop(0, per, stage_one, 0)

    for q in range(n):
        value = mid[q]
        high = value.astype(jnp.bfloat16)
        low = (value - high.astype(jnp.float32)).astype(jnp.bfloat16)
        dot = functools.partial(
            lax.dot_general,
            dimension_numbers=(((1,), (1,)), ((), ())),
            preferred_element_type=jnp.float32,
        )
        total = dot(whi_ref[...], high) + (dot(whi_ref[...], low) + dot(wlo_ref[...], high))
        spread[pl.ds(q, width, stride=n), :] = total

    def turn(owner):
        start = pl.multiple_of(owner * width, width)
        block = spread[pl.ds(start, width), :].T
        for c in range(chunks):
            for part_index in range(2):
                for a in range(per):
                    r0 = (c * 2 + part_index) * rows + a * sub
                    for h in range(halves):
                        units[(c * per + a) * halves + h, part_index] = block[
                            r0 : r0 + sub, h * LANES : (h + 1) * LANES
                        ]
        base = (flat - me) + owner
        for i in range(slots):
            send[owner, i] = units[table[base, 0, i]]

    def send_second(i, carry):
        t = turned(i)
        peer = lax.rem(me + t, n)
        turn(peer)
        second(t).start()
        own_rest(peer).start()
        return carry

    lax.fori_loop(0, n - 1, send_second, 0)
    turn(me)
    own_out().start()
    own_rest(me).start()
    own_out().wait()

    def drain(i, carry):
        own_rest(i).wait()
        return carry

    lax.fori_loop(0, n, drain, 0)

    def quiet(i, carry):
        tell(i).wait_send()
        return carry

    lax.fori_loop(1, everyone, quiet, 0)

    def finish(t, carry):
        for c in range(chunks):
            first(c, t).wait_send()
        second(t).wait_send()
        second(t).wait_recv()
        return carry

    lax.fori_loop(1, n, finish, 0)


def rest_kernel(n, rest_ref, out_ref, s1, r1, own):
    me = lax.axis_index("col")
    barrier = pltpu.get_barrier_semaphore()

    def greet(t, carry):
        pl.semaphore_signal(
            barrier, inc=1, device_id={"col": lax.rem(me + t, n)}, device_id_type=MESH
        )
        return carry

    lax.fori_loop(1, n, greet, 0)
    mine = pltpu.make_async_copy(rest_ref.at[me], out_ref.at[me], own)
    mine.start()
    pl.semaphore_wait(barrier, n - 1)

    def copy(t):
        peer = lax.rem(me + t, n)
        return pltpu.make_async_remote_copy(
            src_ref=rest_ref.at[peer],
            dst_ref=out_ref.at[me],
            send_sem=s1.at[t],
            recv_sem=r1.at[t],
            device_id={"col": peer},
            device_id_type=MESH,
        )

    def begin(t, carry):
        copy(t).start()
        return carry

    def end(t, carry):
        copy(t).wait()
        return carry

    lax.fori_loop(1, n, begin, 0)
    lax.fori_loop(1, n, end, 0)
    mine.wait()


def unpack_kernel(n, blocks, sub, halves, keep, on_ref, band_ref, gain_ref, got_ref, more_ref, out_ref):
    rank = jnp.int32(0)
    a = pl.program_id(0)
    slots = blocks * halves
    for u in range(slots):
        rank = rank + jnp.where(u < a * halves, on_ref[u // halves, u % halves], 0)
    for h in range(halves):
        on = on_ref[a, h]
        gain = gain_ref[band_ref[a, h]]
        cols = pl.ds(h * LANES, LANES)

        def take(ref, slot):
            for d in range(n):
                for part_index in range(2):
                    value = ref[d, slot, part_index]
                    out_ref[part_index, 0, d, :, cols] = value * gain

        @pl.when((on != 0) & (rank < keep))
        def _():
            take(got_ref, rank)

        @pl.when((on != 0) & (rank >= keep))
        def _():
            take(more_ref, rank - keep)

        @pl.when(on == 0)
        def _():
            out_ref[:, 0, :, :, cols] = jnp.zeros((2, n, sub, LANES), jnp.float32)

        rank = rank + on


def tables(n, width):
    length = n * width
    k0 = np.arange(n)[:, None] * np.arange(width)[None, :]
    angle = 2.0 * np.pi * (k0 % length) / length
    twiddle = np.stack([np.cos(angle), -np.sin(angle)]).astype(np.float32)
    k1 = np.arange(width)[:, None] * np.arange(width)[None, :]
    angle = 2.0 * np.pi * (k1 % width) / width
    table = np.concatenate([np.cos(angle), -np.sin(angle)], axis=1) / math.sqrt(length)
    high = table.astype(np.float32).astype(ml_dtypes.bfloat16)
    low = (table - high.astype(np.float64)).astype(np.float32).astype(ml_dtypes.bfloat16)
    return jnp.asarray(twiddle), jnp.asarray(high), jnp.asarray(low)


def packed(slab, block_on, block_band, band_gain):
    n, groups = lax.axis_size("col"), lax.axis_size("groups")
    _, rows_total, width = slab.shape
    blocks, halves = rows_total // BLOCK, width // LANES
    sub = BLOCK // n
    chunks = 2
    per = blocks // chunks
    slots = blocks * halves
    keep = 3 * slots // 4
    sem = pltpu.SemaphoreType.DMA
    anywhere = pl.BlockSpec(memory_space=pl.ANY)
    vmem = pl.BlockSpec(memory_space=pltpu.VMEM)
    smem = pl.BlockSpec(memory_space=pltpu.SMEM)
    f32 = jnp.float32
    unit = (2, sub, LANES)
    everyone = n * groups
    got, rest, flag = pl.pallas_call(
        functools.partial(packed_kernel, n, groups, chunks, blocks, sub, halves, keep),
        out_shape=(
            jax.ShapeDtypeStruct((n, keep) + unit, f32),
            jax.ShapeDtypeStruct((n, slots - keep) + unit, f32),
            jax.ShapeDtypeStruct((1, 1), jnp.int32),
        ),
        in_specs=[anywhere, smem, vmem, vmem, vmem],
        out_specs=(anywhere, anywhere, smem),
        scratch_shapes=[
            pltpu.VMEM((chunks, n, 2, per, sub, width), f32),
            pltpu.VMEM((n, 2 * blocks * sub, 2 * width), f32),
            pltpu.VMEM((n * width, 2 * blocks * sub), f32),
            pltpu.VMEM((slots,) + unit, f32),
            pltpu.VMEM((n, slots) + unit, f32),
            pltpu.VMEM((everyone, 1, LANES), jnp.int32),
            pltpu.SMEM((everyone, 1, LANES), jnp.int32),
            sem((chunks, n)),
            sem((chunks, n)),
            sem((n,)),
            sem((n,)),
            sem((everyone,)),
            sem((everyone,)),
            sem((chunks,)),
            sem,
            sem((n,)),
            sem,
        ],
        compiler_params=pltpu.CompilerParams(
            collective_id=1, has_side_effects=True, vmem_limit_bytes=40 * 1024 * 1024
        ),
    )(slab.reshape(2, blocks, n, sub, width), block_on, *tables(n, width))

    def fetch_rest(rest):
        return pl.pallas_call(
            functools.partial(rest_kernel, n),
            out_shape=jax.ShapeDtypeStruct(rest.shape, f32),
            in_specs=[anywhere],
            out_specs=anywhere,
            scratch_shapes=[sem((n,)), sem((n,)), sem],
            compiler_params=pltpu.CompilerParams(collective_id=2, has_side_effects=True),
        )(rest)

    more = lax.cond(flag[0, 0] > keep, fetch_rest, lambda rest: rest, rest)
    out = pl.pallas_call(
        functools.partial(unpack_kernel, n, blocks, sub, halves, keep),
        out_shape=jax.ShapeDtypeStruct((2, blocks, n, sub, width), f32),
        grid=(blocks,),
        in_specs=[smem, smem, smem, vmem, vmem],
        out_specs=pl.BlockSpec((2, 1, n, sub, width), lambda a: (0, a, 0, 0, 0)),
        compiler_params=pltpu.CompilerParams(vmem_limit_bytes=16 * 1024 * 1024),
    )(block_on, block_band, band_gain, got, more)
    return out.reshape(slab.shape)


def shards(slab, block_on, block_band, band_gain):
    n = lax.axis_size("col")
    _, rows_total, width = slab.shape
    if BLOCK % (8 * n) == 0 and rows_total % (2 * BLOCK) == 0:
        return packed(slab, block_on, block_band, band_gain)
    spectrum = transform(slab, n)
    choose = (block_band[..., None] == jnp.arange(band_gain.shape[0], dtype=jnp.int32)).astype(
        jnp.float32
    )
    weight = block_on.astype(jnp.float32) * jnp.sum(choose * band_gain, axis=-1)
    row_blocks = rows_total // BLOCK
    col_blocks = width // BLOCK
    masked = (
        spectrum.reshape(2, row_blocks, BLOCK, col_blocks, BLOCK) * weight[None, :, None, :, None]
    )
    return masked.reshape(2, rows_total, width)


def solution(mesh):
    placed = (P(None, "groups", "col"), P("groups", "col"), P("groups", "col"), P())
    return jax.shard_map(
        shards, mesh=mesh, in_specs=placed, out_specs=P(None, "groups", "col"), check_vma=False
    )
```

```python
import functools
import math

import jax
import jax.numpy as jnp
import ml_dtypes
import numpy as np
from jax import lax
from jax.experimental import pallas as pl
from jax.experimental.pallas import tpu as pltpu
from jax.sharding import PartitionSpec as P

BLOCK = 128
LANES = 128
MESH = pl.DeviceIdType.MESH


def butterflies(planes):
    count = len(planes)
    if count == 1:
        return planes
    even = butterflies(planes[0::2])
    odd = butterflies(planes[1::2])
    low, high = [], []
    for k in range(count // 2):
        er, ei = even[k]
        xr, xi = odd[k]
        if k == 0:
            tr, ti = xr, xi
        elif 4 * k == count:
            tr, ti = xi, -xr
        else:
            c = math.cos(2.0 * math.pi * k / count)
            s = -math.sin(2.0 * math.pi * k / count)
            if 8 * k == count:
                tr, ti = c * (xr + xi), c * (xi - xr)
            elif 8 * k == 3 * count:
                tr, ti = s * (xr - xi), s * (xr + xi)
            else:
                tr, ti = c * xr - s * xi, c * xi + s * xr
        low.append((er + tr, ei + ti))
        high.append((er - tr, ei - ti))
    return low + high


def kernel(
    n, chunks, rows, x_ref, tw_ref, whi_ref, wlo_ref, out_ref,
    recv, mid, spread, done, s1, r1, s2, r2, own1, own2,
):
    me = lax.axis_index("col")
    rows_here = chunks * rows
    width = x_ref.shape[2]

    barrier = pltpu.get_barrier_semaphore()

    def greet(t, carry):
        pl.semaphore_signal(
            barrier, inc=1, device_id={"col": lax.rem(me + t, n)}, device_id_type=MESH
        )
        return carry

    lax.fori_loop(1, n, greet, 0)

    def part_of(ref, owner, c):
        start = pl.multiple_of(owner * rows_here + c * rows, rows)
        return ref.at[:, pl.ds(start, rows), :]

    def first(c, t):
        peer = lax.rem(me + t, n)
        return pltpu.make_async_remote_copy(
            src_ref=part_of(x_ref, peer, c),
            dst_ref=recv.at[c, me],
            send_sem=s1.at[c, t],
            recv_sem=r1.at[c, t],
            device_id={"col": peer},
            device_id_type=MESH,
        )

    def second(c, t):
        peer = lax.rem(me + t, n)
        return pltpu.make_async_remote_copy(
            src_ref=done.at[c, peer],
            dst_ref=part_of(out_ref, me, c),
            send_sem=s2.at[c, t],
            recv_sem=r2.at[c, t],
            device_id={"col": peer},
            device_id_type=MESH,
        )

    def own_in(c):
        return pltpu.make_async_copy(part_of(x_ref, me, c), recv.at[c, me], own1.at[c])

    def own_out(c):
        return pltpu.make_async_copy(done.at[c, me], part_of(out_ref, me, c), own2.at[c])

    for c in range(chunks):
        own_in(c).start()
    pl.semaphore_wait(barrier, n - 1)
    for c in range(chunks):

        def send_first(t, carry, c=c):
            first(c, t).start()
            return carry

        lax.fori_loop(1, n, send_first, 0)

    for c in range(chunks):
        own_in(c).wait()

        def take_first(t, carry, c=c):
            first(c, t).wait_recv()
            return carry

        lax.fori_loop(1, n, take_first, 0)

        def stage_one(g, carry, c=c):
            r0 = pl.multiple_of(g * 8, 8)
            for h in range(width // LANES):
                cols = pl.ds(h * LANES, LANES)
                planes = [
                    (recv[c, d, 0, pl.ds(r0, 8), cols], recv[c, d, 1, pl.ds(r0, 8), cols])
                    for d in range(n)
                ]
                for q, (ar, ai) in enumerate(butterflies(planes)):
                    if q == 0:
                        br, bi = ar, ai
                    else:
                        tr = tw_ref[0, pl.ds(q, 1), cols]
                        ti = tw_ref[1, pl.ds(q, 1), cols]
                        br = ar * tr - ai * ti
                        bi = ar * ti + ai * tr
                    right = pl.ds(width + h * LANES, LANES)
                    mid[q, pl.ds(r0, 8), cols] = br
                    mid[q, pl.ds(r0, 8), right] = -bi
                    mid[q, pl.ds(rows + r0, 8), cols] = bi
                    mid[q, pl.ds(rows + r0, 8), right] = br
            return carry

        lax.fori_loop(0, rows // 8, stage_one, 0)

        def stage_two(q, carry):
            value = mid[q]
            high = value.astype(jnp.bfloat16)
            low = (value - high.astype(jnp.float32)).astype(jnp.bfloat16)
            nt = (((1,), (1,)), ((), ()))
            dot = functools.partial(
                lax.dot_general, dimension_numbers=nt, preferred_element_type=jnp.float32
            )
            total = dot(whi_ref[...], high) + (dot(whi_ref[...], low) + dot(wlo_ref[...], high))
            spread[pl.ds(q, width, stride=n), pl.ds(0, 2 * rows)] = total
            return carry

        if n <= 16:
            for q in range(n):
                stage_two(q, 0)
        else:
            lax.fori_loop(0, n, stage_two, 0)

        def turn(owner):
            start = pl.multiple_of(owner * width, width)
            block = spread[pl.ds(start, width), :].T
            done[c, owner, 0] = block[:rows]
            done[c, owner, 1] = block[rows : 2 * rows]

        def send_second(t, carry, c=c):
            turn(lax.rem(me + t, n))
            second(c, t).start()
            return carry

        lax.fori_loop(1, n, send_second, 0)
        turn(me)
        own_out(c).start()

    for c in range(chunks):
        own_out(c).wait()

        def finish(t, carry, c=c):
            first(c, t).wait_send()
            second(c, t).wait_send()
            second(c, t).wait_recv()
            return carry

        lax.fori_loop(1, n, finish, 0)


def transform(slab, n):
    _, rows_total, width = slab.shape
    length = width * n
    rows_here = rows_total // n
    chunks = 2 if rows_here % 16 == 0 else 1
    rows = rows_here // chunks
    lanes = max(LANES, 2 * rows)
    k0 = np.arange(n)[:, None] * np.arange(width)[None, :]
    angle = 2.0 * np.pi * (k0 % length) / length
    twiddle = np.stack([np.cos(angle), -np.sin(angle)]).astype(np.float32)
    k1 = np.arange(width)[:, None] * np.arange(width)[None, :]
    angle = 2.0 * np.pi * (k1 % width) / width
    table = np.concatenate([np.cos(angle), -np.sin(angle)], axis=1) / math.sqrt(length)
    table_high = table.astype(np.float32).astype(ml_dtypes.bfloat16)
    table_low = (table - table_high.astype(np.float64)).astype(np.float32)
    table_low = table_low.astype(ml_dtypes.bfloat16)
    sem = pltpu.SemaphoreType.DMA
    return pl.pallas_call(
        functools.partial(kernel, n, chunks, rows),
        out_shape=jax.ShapeDtypeStruct(slab.shape, jnp.float32),
        in_specs=[pl.BlockSpec(memory_space=pl.ANY)]
        + [pl.BlockSpec(memory_space=pltpu.VMEM)] * 3,
        out_specs=pl.BlockSpec(memory_space=pl.ANY),
        scratch_shapes=[
            pltpu.VMEM((chunks, n, 2, rows, width), jnp.float32),
            pltpu.VMEM((n, 2 * rows, 2 * width), jnp.float32),
            pltpu.VMEM((length + n, lanes), jnp.float32),
            pltpu.VMEM((chunks, n, 2, rows, width), jnp.float32),
            sem((chunks, n)),
            sem((chunks, n)),
            sem((chunks, n)),
            sem((chunks, n)),
            sem((chunks,)),
            sem((chunks,)),
        ],
        compiler_params=pltpu.CompilerParams(
            collective_id=0, has_side_effects=True, vmem_limit_bytes=48 * 1024 * 1024
        ),
    )(slab, jnp.asarray(twiddle), jnp.asarray(table_high), jnp.asarray(table_low))


def shards(slab, block_on, block_band, band_gain):
    n = lax.axis_size("col")
    _, rows_total, width = slab.shape
    spectrum = transform(slab, n)
    choose = (block_band[..., None] == jnp.arange(band_gain.shape[0], dtype=jnp.int32)).astype(
        jnp.float32
    )
    weight = block_on.astype(jnp.float32) * jnp.sum(choose * band_gain, axis=-1)
    row_blocks = rows_total // BLOCK
    col_blocks = width // BLOCK
    masked = (
        spectrum.reshape(2, row_blocks, BLOCK, col_blocks, BLOCK) * weight[None, :, None, :, None]
    )
    return masked.reshape(2, rows_total, width)


def solution(mesh):
    placed = (P(None, "groups", "col"), P("groups", "col"), P("groups", "col"), P())
    return jax.shard_map(
        shards, mesh=mesh, in_specs=placed, out_specs=P(None, "groups", "col"), check_vma=False
    )
```
